128 devices in a mesh: ctx: 16 (over z, y_lo, core), uly: 8 (over y_hi, x).
Axes of the slice: x: 4, y: 4 (y_hi: 2, y_lo: 2; y = y_hi * 2 + y_lo), z: 4, core: 2. Of those that a mesh axis runs over, the one named last changes fastest.
Arguments:
- query_rows: bfloat16 [16384, 5120], P(('ctx', 'uly')), may hold values from -256 to 256
- key_rows: bfloat16 [2048, 5120], P(('ctx', 'uly')), may hold values from -32 to 32
- value_rows: bfloat16 [2048, 5120], P(('ctx', 'uly')), may hold values from -6 to 6
- query_tangent: bfloat16 [16384, 5120], P(('ctx', 'uly')), may hold values from -6 to 6
- key_tangent: bfloat16 [2048, 5120], P(('ctx', 'uly')), may hold values from -6 to 6
- value_tangent: bfloat16 [2048, 5120], P(('ctx', 'uly')), may hold values from -6 to 6
Outputs:
- attended: bfloat16 [16384, 5120], P(('ctx', 'uly'))
- attended_tangent: bfloat16 [16384, 5120], P(('ctx', 'uly'))
The draws below stay inside these ranges and needn't reach their ends.
All inputs are finite; a program needn't handle non-finite values.
Results may differ from the reference program's by a relative error of at most 0.0088.
Values may be sent and summed in bfloat16 or wider, within the bound.
A program may use at most 128 MiB of HBM per device.

```python
import math
import jax
import jax.numpy as jnp
from jax import lax

HD = 128
HEADS = 40
QTOK = 16384
KTOK = 2048


def row_scales(scale_key, count, lowest, highest):
    return jnp.exp(jax.random.uniform(scale_key, (count, 1), jnp.float32, math.log(lowest), math.log(highest)))


def draw_key_rows(key, part):
    key = jax.random.fold_in(key, 11)
    scale_key, noise_key = jax.random.split(key)
    jitter = jax.random.truncated_normal(noise_key, -6.0, 6.0, (KTOK, HEADS * HD), jnp.float32)
    return (row_scales(scale_key, KTOK, 0.3, 5.0) * jitter).astype(jnp.bfloat16)


def draw_query_rows(key, part):
    key = jax.random.fold_in(key, 12)
    scale_key, noise_key = jax.random.split(key)
    scales = row_scales(scale_key, QTOK, 0.3, 5.0)
    drawn = jax.random.truncated_normal(noise_key, -6.0, 6.0, (QTOK, HEADS * HD), jnp.float32)
    return (scales * drawn).astype(jnp.bfloat16)


def draw_key_tangent(key, part):
    key = jax.random.fold_in(key, 13)
    return jax.random.truncated_normal(key, -6.0, 6.0, (KTOK, HEADS * HD), jnp.float32).astype(jnp.bfloat16)


def block_levels(own_key, shape, shards, smallest, largest):
    level, own = 1.0, jax.random.fold_in(own_key, 6)
    for axis_at, shards_of in shards:
        heights = jnp.exp(jax.random.uniform(jax.random.fold_in(own, axis_at), (shards_of,), jnp.float32, smallest / len(shards), largest / len(shards)))
        level = level * jnp.repeat(heights, shape[axis_at] // shards_of).reshape([-1 if axis == axis_at else 1 for axis in range(len(shape))])
    return level


def centred(stream_key, dims, scale, bound, cuts=(), held_as=jnp.bfloat16):
    level = block_levels(stream_key, dims, cuts, -0.22, 0.18) if cuts else 1.0
    array = jax.random.normal(stream_key, dims, jnp.float32) * scale * level
    return jnp.minimum(jnp.maximum(array, -bound), bound).astype(held_as)


def setup_inputs(seed: int = 0) -> dict:
    arg_keys = jax.random.split(jax.random.key(seed), 7)
    return {
        "query_rows": draw_query_rows(jax.random.fold_in(arg_keys[6], 71), 0),
        "key_rows": draw_key_rows(jax.random.fold_in(arg_keys[6], 71), 0),
        "value_rows": centred(arg_keys[2], (KTOK, HEADS * HD), 1.0, 6.0, ((0, 128),)),
        "query_tangent": centred(arg_keys[3], (QTOK, HEADS * HD), 1.0, 6.0, ((0, 128),)),
        "key_tangent": draw_key_tangent(jax.random.fold_in(arg_keys[6], 71), 0),
        "value_tangent": centred(arg_keys[5], (KTOK, HEADS * HD), 1.0, 6.0, ((0, 128),)),
    }


def widened(matrix):
    return matrix.astype(jnp.float32)

def product(left, right):
    return jnp.dot(widened(left), widened(right), precision=lax.Precision.HIGHEST)

def attend_head(head_block):
    query_head, key_head, value_head, dquery_head, dkey_head, dvalue_head = head_block
    score_scale = 1.0 / math.sqrt(HD)
    scores = product(query_head, key_head.T) * score_scale
    highest = lax.optimization_barrier(jnp.max(scores, axis=1, keepdims=True))
    weights = jnp.exp(scores - highest)
    total = lax.optimization_barrier(jnp.sum(weights, axis=1, keepdims=True))
    weights_rounded = lax.optimization_barrier(weights.astype(jnp.bfloat16))
    mixed = product(weights_rounded, value_head) / total
    score_tangent = (product(dquery_head, key_head.T) + product(query_head, dkey_head.T)) * score_scale
    weighted = weights * score_tangent
    moment = lax.optimization_barrier(jnp.sum(weighted, axis=1, keepdims=True))
    product_rounded = lax.optimization_barrier(weighted.astype(jnp.bfloat16))
    tangent = (product(product_rounded, value_head) + product(weights_rounded, dvalue_head) - mixed * moment) / total
    return (mixed.astype(jnp.bfloat16), tangent.astype(jnp.bfloat16))

def by_heads(matrix):
    return matrix.reshape(matrix.shape[0], HEADS, HD).transpose(1, 0, 2)

def to_columns(stacked):
    return stacked.transpose(1, 0, 2).reshape(stacked.shape[1], HEADS * HD)

def reference(query_rows, key_rows, value_rows, query_tangent, key_tangent, value_tangent):
    inputs = (by_heads(query_rows), by_heads(key_rows), by_heads(value_rows), by_heads(query_tangent), by_heads(key_tangent), by_heads(value_tangent))
    mixed_all, tangent_all = lax.map(attend_head, inputs)
    return (to_columns(mixed_all), to_columns(tangent_all))
```

```python
import functools
import math

import jax
import jax.numpy as jnp
from jax import lax
from jax.experimental import pallas as pl
from jax.experimental.pallas import tpu as pltpu
from jax.sharding import PartitionSpec as P

HD = 128
SLOTS = 5
GROUP = 8
QROWS = 128
KROWS = 16
BLOCK = GROUP * KROWS
QUERIES = GROUP * QROWS
KEYS = 2048
COLS = 5120
TILE = 256
SCALE = 1.0 / math.sqrt(HD)
SCALE_LOG2 = SCALE * math.log2(math.e)
MESH = pl.DeviceIdType.MESH

LAYOUT = ((0, 1, 2, 0),) * SLOTS


def scores_of(left, right):
    return lax.dot_general(left, right, (((1,), (1,)), ((), ())), preferred_element_type=jnp.float32)


def mix(left, right):
    return jnp.dot(left, right, preferred_element_type=jnp.float32)


class Place:
    def __init__(self, slot, xyz, core):
        ring, pair, keys, shift = LAYOUT[slot]
        self.order, self.shift, self.core, self.slot = (ring, pair, keys), shift, core, slot
        self.a = xyz[ring]
        self.b = lax.rem(xyz[pair] + shift, 4)
        self.c = xyz[keys]
        self.member = self.a + 4 * lax.rem(self.b, 2)
        self.kind = self.kind_of(self.a, self.b)
        self.block = self.block_of(self.b, self.c, core)

    def kind_of(self, a, b):
        return a + 4 * lax.rem(lax.rem(b, 2) + lax.div(b, 2), 2)

    def block_of(self, b, c, core):
        return (c * 2 + lax.div(b, 2)) * 2 + core

    def device(self, a, b, c, core):
        xyz = [None] * 3
        for axis, at in zip(self.order, (a, lax.rem(b + 4 - self.shift, 4), c)):
            xyz[axis] = at
        x, y, z = xyz
        return (z * 4 + lax.rem(y, 2) * 2 + core, lax.div(y, 2) * 4 + x)

    def peers(self):
        found = []
        for da in range(4):
            for db in range(2):
                if da or db:
                    a = lax.rem(self.a + da, 4)
                    b = self.b + (1 - 2 * lax.rem(self.b, 2)) * db
                    found.append((self.device(a, b, self.c, self.core), a + 4 * lax.rem(b, 2), self.kind_of(a, b)))
        return found

    def across(self):
        return self.device(self.a, 3 - self.b, self.c, self.core)

    def along(self, step):
        return self.device(self.a, self.b, lax.rem(self.c + step, 4), self.core)

    def twin(self):
        return self.device(self.a, self.b, self.c, 1 - self.core)


def columns(head):
    return pl.ds(pl.multiple_of(head * HD, HD), HD)


def rows(start, size):
    return pl.ds(pl.multiple_of(start, 16), size)


def send(src, dst, send_sem, recv_sem, device):
    pltpu.make_async_remote_copy(
        src_ref=src, dst_ref=dst, send_sem=send_sem, recv_sem=recv_sem, device_id=device, device_id_type=MESH
    ).start()


def wait_bytes(ref, sem):
    pltpu.make_async_copy(ref, ref, sem).wait()


def kernel(
    q_ref, k_ref, v_ref, dq_ref, dk_ref, dv_ref, out_ref,
    q_own, k_own, q_all, k_all, o_all,
    stage_sem, q_send, q_recv, k1_send, k1_recv, k2_send, across_recv, along_recv, twin_recv, o_send, o_recv,
):
    ctx, uly = lax.axis_index("ctx"), lax.axis_index("uly")
    core = lax.rem(ctx, 2)
    xyz = (lax.rem(uly, 4), lax.div(uly, 4) * 2 + lax.rem(lax.div(ctx, 2), 2), lax.div(ctx, 4))
    places = [Place(slot, xyz, core) for slot in range(SLOTS)]

    staged = [
        pltpu.make_async_copy(ref, k_own.at[at], stage_sem.at[at]) for at, ref in enumerate((k_ref, dk_ref, v_ref, dv_ref))
    ] + [pltpu.make_async_copy(ref, q_own.at[at], stage_sem.at[4 + at]) for at, ref in enumerate((q_ref, dq_ref))]
    for copy in staged:
        copy.start()

    barrier = pltpu.get_barrier_semaphore()
    partners = [places[0].twin()]
    for slot, place in enumerate(places):
        if LAYOUT[slot] not in LAYOUT[:slot]:
            partners += [device for device, _, _ in place.peers()]
            partners += [place.across()] + [place.along(step) for step in (1, 2, 3)]
    for device in partners:
        pl.semaphore_signal(barrier, inc=1, device_id=device, device_id_type=MESH)
    pl.semaphore_wait(barrier, len(partners))
    for copy in staged:
        copy.wait()

    def send_keys(slot):
        place = places[slot]
        there = k_all.at[slot, :, rows(place.block * BLOCK + place.member * KROWS, KROWS), :]
        for device, _, kind in place.peers():
            send(k_own.at[:, :, columns(slot * GROUP + kind)], there, k1_send.at[slot], k1_recv.at[slot], device)
        pltpu.make_async_copy(k_own.at[:, :, columns(slot * GROUP + place.kind)], there, k1_recv.at[slot]).start()

    def send_queries(slot):
        place = places[slot]
        there = q_all.at[slot, :, rows(place.member * QROWS, QROWS), :]
        for device, _, kind in place.peers():
            send(q_own.at[:, :, columns(slot * GROUP + kind)], there, q_send.at[slot], q_recv.at[slot], device)
        pltpu.make_async_copy(q_own.at[:, :, columns(slot * GROUP + place.kind)], there, q_recv.at[slot]).start()

    def block_ref(slot, block):
        return k_all.at[slot, :, rows(block * BLOCK, BLOCK), :]

    def to_twin(slot, block):
        ref = block_ref(slot, block)
        send(ref, ref, k2_send.at[slot], twin_recv.at[slot], places[slot].twin())

    def along_all(slot, block, which):
        ref = block_ref(slot, block)
        for step in (1, 3, 2):
            send(ref, ref, k2_send.at[slot], along_recv.at[slot, which, step - 1], places[slot].along(step))
        to_twin(slot, block)

    def own_block(slot):
        place = places[slot]
        ref = block_ref(slot, place.block)
        wait_bytes(ref, k1_recv.at[slot])
        send(ref, ref, k2_send.at[slot], across_recv.at[slot], place.across())
        along_all(slot, place.block, 0)

    def across_block(slot):
        place = places[slot]
        block = place.block_of(3 - place.b, place.c, core)
        wait_bytes(block_ref(slot, block), across_recv.at[slot])
        along_all(slot, block, 1)

    def along_blocks(slot, which):
        place = places[slot]
        b = 3 - place.b if which else place.b
        for step in (1, 3, 2):
            block = place.block_of(b, lax.rem(place.c + 4 - step, 4), core)
            wait_bytes(block_ref(slot, block), along_recv.at[slot, which, step - 1])
            to_twin(slot, block)

    def attend(slot):
        def tile(at, _):
            here = rows(at * TILE, TILE)
            query, dquery = q_all[slot, 0, here, :], q_all[slot, 1, here, :]
            key, dkey = k_all[slot, 0], k_all[slot, 1]
            value, dvalue = k_all[slot, 2], k_all[slot, 3]
            scores = scores_of(query, key) * SCALE_LOG2
            tangents = scores_of(jnp.concatenate([dquery, query], 1), jnp.concatenate([key, dkey], 1))
            highest = jnp.max(scores, axis=1, keepdims=True)
            weights = jnp.exp2(scores - highest)
            total = jnp.sum(weights, axis=1, keepdims=True)
            weights_rounded = weights.astype(jnp.bfloat16)
            product = weights * (tangents * SCALE)
            moment = jnp.sum(product, axis=1, keepdims=True)
            both = mix(weights_rounded, jnp.concatenate([value, dvalue], 1))
            mixed = both[:, :HD] / total
            tangent = (mix(product.astype(jnp.bfloat16), value) + both[:, HD:] - mixed * moment) / total
            o_all[slot, 0, here, :] = mixed.astype(jnp.bfloat16)
            o_all[slot, 1, here, :] = tangent.astype(jnp.bfloat16)
            return 0

        lax.fori_loop(0, QUERIES // TILE, tile, 0)

    def send_outputs(slot):
        place = places[slot]
        there = out_ref.at[:, :, columns(slot * GROUP + place.kind)]
        for device, member, _ in place.peers():
            send(o_all.at[slot, :, rows(member * QROWS, QROWS), :], there, o_send.at[slot], o_recv, device)
        pltpu.make_async_copy(o_all.at[slot, :, rows(place.member * QROWS, QROWS), :], there, o_recv).start()

    for slot in range(SLOTS):
        send_keys(slot)
    send_queries(0)
    own_block(0)
    across_block(0)
    send_queries(1)
    own_block(1)
    along_blocks(0, 0)
    along_blocks(0, 1)
    for slot in range(SLOTS):
        if slot + 1 < SLOTS:
            across_block(slot + 1)
        if slot + 2 < SLOTS:
            send_queries(slot + 2)
            own_block(slot + 2)
        wait_bytes(k_all.at[slot, :, : KEYS // 2, :], twin_recv.at[slot])
        wait_bytes(q_all.at[slot], q_recv.at[slot])
        attend(slot)
        send_outputs(slot)
        if slot + 1 < SLOTS:
            along_blocks(slot + 1, 0)
            along_blocks(slot + 1, 1)

    for slot in range(SLOTS):
        wait_bytes(k_all.at[slot, :, : 7 * KROWS, :], k1_send.at[slot])
        wait_bytes(q_all.at[slot, :, : 7 * QROWS, :], q_send.at[slot])
        wait_bytes(k_all.at[slot, :, : 15 * BLOCK, :], k2_send.at[slot])
        wait_bytes(o_all.at[slot, :, : 7 * QROWS, :], o_send.at[slot])
    wait_bytes(out_ref, o_recv)


def on_device(query_rows, key_rows, value_rows, query_tangent, key_tangent, value_tangent):
    dma = pltpu.SemaphoreType.DMA
    out = pl.pallas_call(
        kernel,
        out_shape=jax.ShapeDtypeStruct((2, QROWS, COLS), jnp.bfloat16),
        in_specs=[pl.BlockSpec(memory_space=pl.ANY)] * 6,
        out_specs=pl.BlockSpec(memory_space=pl.ANY),
        scratch_shapes=[
            pltpu.VMEM((2, QROWS, COLS), jnp.bfloat16),
            pltpu.VMEM((4, KROWS, COLS), jnp.bfloat16),
            pltpu.VMEM((SLOTS, 2, QUERIES, HD), jnp.bfloat16),
            pltpu.VMEM((SLOTS, 4, KEYS, HD), jnp.bfloat16),
            pltpu.VMEM((SLOTS, 2, QUERIES, HD), jnp.bfloat16),
            dma((6,)),
            dma((SLOTS,)),
            dma((SLOTS,)),
            dma((SLOTS,)),
            dma((SLOTS,)),
            dma((SLOTS,)),
            dma((SLOTS,)),
            dma((SLOTS, 2, 3)),
            dma((SLOTS,)),
            dma((SLOTS,)),
            dma(()),
        ],
        compiler_params=pltpu.CompilerParams(collective_id=0, has_side_effects=True, vmem_limit_bytes=56 * 2**20),
        cost_estimate=pl.CostEstimate(flops=16_000_000_000, bytes_accessed=6_000_000, transcendentals=10_500_000),
        name="tangent_attention",
    )(query_rows, key_rows, value_rows, query_tangent, key_tangent, value_tangent)
    return out[0], out[1]


def solution(mesh):
    whole = P(("ctx", "uly"), None)
    return jax.shard_map(on_device, mesh=mesh, in_specs=(whole,) * 6, out_specs=(whole, whole), check_vma=False)
```

```python
import functools
import math

import jax
import jax.numpy as jnp
from jax import lax
from jax.experimental import pallas as pl
from jax.experimental.pallas import tpu as pltpu
from jax.sharding import PartitionSpec as P

HD = 128
SLOTS = 5
GROUP = 8
QROWS = 128
KROWS = 16
BLOCK = GROUP * KROWS
QUERIES = GROUP * QROWS
KEYS = 2048
COLS = 5120
TILE = 256
SCALE = 1.0 / math.sqrt(HD)
SCALE_LOG2 = SCALE * math.log2(math.e)
MESH = pl.DeviceIdType.MESH

LAYOUT = (
    (0, 1, 2, 0),
    (1, 2, 0, 0),
    (2, 0, 1, 0),
    (0, 1, 2, 1),
    (1, 2, 0, 1),
)

PLAN = (
    (" ".join(("keys0 keys1 keys2 keys3", "keys4 queries0 own0 own1", "own2 own3 own4 cross0", "cross1 near0 cross2 cross3", "near1 cross4 far0 near2", "near3 far1")),),
    ("queries1 ready0", "near4", "queries2 far2", "far3",),
    ("queries3 ready1", "far4", "queries4", "",),
    ("ready2", "", "", "",),
    ("ready3", "", "", "",),
    ("ready4", "", "", "",),
)


def scores_of(left, right):
    return lax.dot_general(left, right, (((1,), (1,)), ((), ())), preferred_element_type=jnp.float32)


def mix(left, right):
    return jnp.dot(left, right, preferred_element_type=jnp.float32)


class Place:
    def __init__(self, slot, xyz, core):
        ring, pair, keys, shift = LAYOUT[slot]
        self.order, self.shift, self.core, self.slot = (ring, pair, keys), shift, core, slot
        self.a = xyz[ring]
        self.b = lax.rem(xyz[pair] + shift, 4)
        self.c = xyz[keys]
        self.member = self.a + 4 * lax.rem(self.b, 2)
        self.kind = self.kind_of(self.a, self.b)
        self.block = self.block_of(self.b, self.c, core)

    def kind_of(self, a, b):
        return a + 4 * lax.rem(lax.rem(b, 2) + lax.div(b, 2), 2)

    def block_of(self, b, c, core):
        return (c * 2 + lax.div(b, 2)) * 2 + core

    def device(self, a, b, c, core):
        xyz = [None] * 3
        for axis, at in zip(self.order, (a, lax.rem(b + 4 - self.shift, 4), c)):
            xyz[axis] = at
        x, y, z = xyz
        return (z * 4 + lax.rem(y, 2) * 2 + core, lax.div(y, 2) * 4 + x)

    def peers(self):
        found = []
        for da in range(4):
            for db in range(2):
                if da or db:
                    a = lax.rem(self.a + da, 4)
                    b = self.b + (1 - 2 * lax.rem(self.b, 2)) * db
                    found.append((self.device(a, b, self.c, self.core), a + 4 * lax.rem(b, 2), self.kind_of(a, b)))
        return found

    def across(self):
        return self.device(self.a, 3 - self.b, self.c, self.core)

    def along(self, step):
        return self.device(self.a, self.b, lax.rem(self.c + step, 4), self.core)

    def twin(self):
        return self.device(self.a, self.b, self.c, 1 - self.core)


def columns(head):
    return pl.ds(pl.multiple_of(head * HD, HD), HD)


def rows(start, size):
    return pl.ds(pl.multiple_of(start, 16), size)


def send(src, dst, send_sem, recv_sem, device):
    pltpu.make_async_remote_copy(
        src_ref=src, dst_ref=dst, send_sem=send_sem, recv_sem=recv_sem, device_id=device, device_id_type=MESH
    ).start()


def wait_bytes(ref, sem):
    pltpu.make_async_copy(ref, ref, sem).wait()


def kernel(
    q_ref, k_ref, v_ref, dq_ref, dk_ref, dv_ref, out_ref,
    q_own, k_own, q_all, k_all, o_all,
    stage_sem, q_send, q_recv, k1_send, k1_recv, k2_send, across_recv, along_recv, twin_recv, o_send, o_recv,
):
    ctx, uly = lax.axis_index("ctx"), lax.axis_index("uly")
    core = lax.rem(ctx, 2)
    xyz = (lax.rem(uly, 4), lax.div(uly, 4) * 2 + lax.rem(lax.div(ctx, 2), 2), lax.div(ctx, 4))
    places = [Place(slot, xyz, core) for slot in range(SLOTS)]

    staged = [
        pltpu.make_async_copy(ref, k_own.at[at], stage_sem.at[at]) for at, ref in enumerate((k_ref, dk_ref, v_ref, dv_ref))
    ] + [pltpu.make_async_copy(ref, q_own.at[at], stage_sem.at[4 + at]) for at, ref in enumerate((q_ref, dq_ref))]
    for copy in staged:
        copy.start()

    barrier = pltpu.get_barrier_semaphore()
    partners = [places[0].twin()]
    for slot, place in enumerate(places):
        if LAYOUT[slot] not in LAYOUT[:slot]:
            partners += [device for device, _, _ in place.peers()]
            partners += [place.across()] + [place.along(step) for step in (1, 2, 3)]
    for device in partners:
        pl.semaphore_signal(barrier, inc=1, device_id=device, device_id_type=MESH)
    pl.semaphore_wait(barrier, len(partners))
    for copy in staged:
        copy.wait()

    def send_keys(slot):
        place = places[slot]
        there = k_all.at[slot, :, rows(place.block * BLOCK + place.member * KROWS, KROWS), :]
        for device, _, kind in place.peers():
            send(k_own.at[:, :, columns(slot * GROUP + kind)], there, k1_send.at[slot], k1_recv.at[slot], device)
        pltpu.make_async_copy(k_own.at[:, :, columns(slot * GROUP + place.kind)], there, k1_recv.at[slot]).start()

    def send_queries(slot):
        place = places[slot]
        there = q_all.at[slot, :, rows(place.member * QROWS, QROWS), :]
        for device, _, kind in place.peers():
            send(q_own.at[:, :, columns(slot * GROUP + kind)], there, q_send.at[slot], q_recv.at[slot], device)
        pltpu.make_async_copy(q_own.at[:, :, columns(slot * GROUP + place.kind)], there, q_recv.at[slot]).start()

    def block_ref(slot, block):
        return k_all.at[slot, :, rows(block * BLOCK, BLOCK), :]

    def to_twin(slot, block):
        ref = block_ref(slot, block)
        send(ref, ref, k2_send.at[slot], twin_recv.at[slot], places[slot].twin())

    def along(slot, block, which, step):
        ref = block_ref(slot, block)
        hop = (1, 3)[which] if step == 2 else step
        send(ref, ref, k2_send.at[slot], along_recv.at[slot, which, step - 1], places[slot].along(hop))

    def own(slot):
        place = places[slot]
        ref = block_ref(slot, place.block)
        wait_bytes(ref, k1_recv.at[slot])
        send(ref, ref, k2_send.at[slot], across_recv.at[slot], place.across())
        along(slot, place.block, 0, 1)
        along(slot, place.block, 0, 3)
        to_twin(slot, place.block)

    def cross(slot):
        place = places[slot]
        block = place.block_of(3 - place.b, place.c, core)
        wait_bytes(block_ref(slot, block), across_recv.at[slot])
        along(slot, block, 1, 3)
        along(slot, block, 1, 1)
        to_twin(slot, block)

    def arrived(slot, which, step):
        place = places[slot]
        b = 3 - place.b if which else place.b
        block = place.block_of(b, lax.rem(place.c + 4 - step, 4), core)
        wait_bytes(block_ref(slot, block), along_recv.at[slot, which, step - 1])
        if step == (1, 3)[which]:
            along(slot, block, which, 2)
        to_twin(slot, block)

    def near(slot):
        arrived(slot, 0, 1)
        arrived(slot, 0, 3)
        arrived(slot, 1, 3)
        arrived(slot, 1, 1)

    def far(slot):
        arrived(slot, 0, 2)
        arrived(slot, 1, 2)

    def ready(slot):
        wait_bytes(k_all.at[slot, :, : KEYS // 2, :], twin_recv.at[slot])
        wait_bytes(q_all.at[slot], q_recv.at[slot])

    steps = {"keys": send_keys, "queries": send_queries, "own": own, "cross": cross, "near": near, "far": far, "ready": ready}

    def follow(plan):
        for step in plan.split():
            steps[step[:-1]](int(step[-1]))

    def attend(slot):
        def tile(at, _):
            for point in range(1, QUERIES // TILE):
                if PLAN[slot + 1][point]:
                    pl.when(at == point)(functools.partial(follow, PLAN[slot + 1][point]))
            here = rows(at * TILE, TILE)
            query, dquery = q_all[slot, 0, here, :], q_all[slot, 1, here, :]
            key, dkey = k_all[slot, 0], k_all[slot, 1]
            value, dvalue = k_all[slot, 2], k_all[slot, 3]
            scores = scores_of(query, key) * SCALE_LOG2
            tangents = scores_of(jnp.concatenate([dquery, query], 1), jnp.concatenate([key, dkey], 1))
            highest = jnp.max(scores, axis=1, keepdims=True)
            weights = jnp.exp2(scores - highest)
            total = jnp.sum(weights, axis=1, keepdims=True)
            weights_rounded = weights.astype(jnp.bfloat16)
            product = weights * (tangents * SCALE)
            both = mix(weights_rounded, jnp.concatenate([value, dvalue], 1))
            mixed = both[:, :HD] / total
            summed = mix(product.astype(jnp.bfloat16), jnp.concatenate([value, jnp.ones_like(value)], 1))
            tangent = (summed[:, :HD] + both[:, HD:] - mixed * summed[:, HD:]) / total
            o_all[slot, 0, here, :] = mixed.astype(jnp.bfloat16)
            o_all[slot, 1, here, :] = tangent.astype(jnp.bfloat16)
            send_outputs(slot, at)
            return 0

        lax.fori_loop(0, QUERIES // TILE, tile, 0)

    def send_outputs(slot, at):
        place = places[slot]
        there = out_ref.at[:, :, columns(slot * GROUP + place.kind)]
        for member in [at * (TILE // QROWS) + part for part in range(TILE // QROWS)]:
            here = o_all.at[slot, :, rows(member * QROWS, QROWS), :]
            device = place.device(lax.rem(member, 4), lax.div(place.b, 2) * 2 + lax.div(member, 4), place.c, core)

            @pl.when(member != place.member)
            def _():
                send(here, there, o_send.at[slot], o_recv, device)

            @pl.when(member == place.member)
            def _():
                pltpu.make_async_copy(here, there, o_recv).start()

    follow(PLAN[0][0])
    for slot in range(SLOTS):
        follow(PLAN[slot + 1][0])
        attend(slot)

    for slot in range(SLOTS):
        wait_bytes(k_all.at[slot, :, : 7 * KROWS, :], k1_send.at[slot])
        wait_bytes(q_all.at[slot, :, : 7 * QROWS, :], q_send.at[slot])
        wait_bytes(k_all.at[slot, :, : 15 * BLOCK, :], k2_send.at[slot])
        wait_bytes(o_all.at[slot, :, : 7 * QROWS, :], o_send.at[slot])
    wait_bytes(out_ref, o_recv)


def on_device(query_rows, key_rows, value_rows, query_tangent, key_tangent, value_tangent):
    dma = pltpu.SemaphoreType.DMA
    out = pl.pallas_call(
        kernel,
        out_shape=jax.ShapeDtypeStruct((2, QROWS, COLS), jnp.bfloat16),
        in_specs=[pl.BlockSpec(memory_space=pl.ANY)] * 6,
        out_specs=pl.BlockSpec(memory_space=pl.ANY),
        scratch_shapes=[
            pltpu.VMEM((2, QROWS, COLS), jnp.bfloat16),
            pltpu.VMEM((4, KROWS, COLS), jnp.bfloat16),
            pltpu.VMEM((SLOTS, 2, QUERIES, HD), jnp.bfloat16),
            pltpu.VMEM((SLOTS, 4, KEYS, HD), jnp.bfloat16),
            pltpu.VMEM((SLOTS, 2, QUERIES, HD), jnp.bfloat16),
            dma((6,)),
            dma((SLOTS,)),
            dma((SLOTS,)),
            dma((SLOTS,)),
            dma((SLOTS,)),
            dma((SLOTS,)),
            dma((SLOTS,)),
            dma((SLOTS, 2, 3)),
            dma((SLOTS,)),
            dma((SLOTS,)),
            dma(()),
        ],
        compiler_params=pltpu.CompilerParams(collective_id=0, has_side_effects=True, vmem_limit_bytes=56 * 2**20),
        cost_estimate=pl.CostEstimate(flops=16_000_000_000, bytes_accessed=6_000_000, transcendentals=10_500_000),
        name="tangent_attention",
    )(query_rows, key_rows, value_rows, query_tangent, key_tangent, value_tangent)
    return out[0], out[1]


def solution(mesh):
    whole = P(("ctx", "uly"), None)
    return jax.shard_map(on_device, mesh=mesh, in_specs=(whole,) * 6, out_specs=(whole, whole), check_vma=False)
```

```python
import functools
import math

import jax
import jax.numpy as jnp
from jax import lax
from jax.experimental import pallas as pl
from jax.experimental.pallas import tpu as pltpu
from jax.sharding import PartitionSpec as P

HD = 128
SLOTS = 5
GROUP = 8
QROWS = 128
KROWS = 16
BLOCK = GROUP * KROWS
QUERIES = GROUP * QROWS
KEYS = 2048
COLS = 5120
TILE = 256
SCALE = 1.0 / math.sqrt(HD)
SCALE_LOG2 = SCALE * math.log2(math.e)
MESH = pl.DeviceIdType.MESH

LAYOUT = (
    (2, 0, 1, 0),
    (1, 2, 0, 0),
    (0, 1, 2, 0),
    (1, 2, 0, 1),
    (0, 1, 2, 1),
)

PLAN = (
    (" ".join(("keys0 keys1 keys2 keys3", "keys4 queries0 own0 own1", "own2 own3 own4 cross0", "cross1 near0 cross2 cross3", "near1 cross4 far0 near2", "near3 far1")),),
    ("queries1 ready0", "near4", "queries2 far2", "far3",),
    ("queries3 ready1", "far4", "queries4", "",),
    ("ready2", "", "", "",),
    ("ready3", "", "", "",),
    ("ready4", "", "", "",),
)


def scores_of(left, right):
    return lax.dot_general(left, right, (((1,), (1,)), ((), ())), preferred_element_type=jnp.float32)


def mix(left, right):
    return jnp.dot(left, right, preferred_element_type=jnp.float32)


class Place:
    def __init__(self, slot, xyz, core):
        ring, pair, keys, shift = LAYOUT[slot]
        self.order, self.shift, self.core, self.slot = (ring, pair, keys), shift, core, slot
        self.a = xyz[ring]
        self.b = lax.rem(xyz[pair] + shift, 4)
        self.c = xyz[keys]
        self.member = self.a + 4 * lax.rem(self.b, 2)
        self.kind = self.kind_of(self.a, self.b)
        self.block = self.block_of(self.b, self.c, core)

    def kind_of(self, a, b):
        return a + 4 * lax.rem(lax.rem(b, 2) + lax.div(b, 2), 2)

    def block_of(self, b, c, core):
        return (c * 2 + lax.div(b, 2)) * 2 + core

    def device(self, a, b, c, core):
        xyz = [None] * 3
        for axis, at in zip(self.order, (a, lax.rem(b + 4 - self.shift, 4), c)):
            xyz[axis] = at
        x, y, z = xyz
        return (z * 4 + lax.rem(y, 2) * 2 + core, lax.div(y, 2) * 4 + x)

    def peers(self):
        found = []
        for da in range(4):
            for db in range(2):
                if da or db:
                    a = lax.rem(self.a + da, 4)
                    b = self.b + (1 - 2 * lax.rem(self.b, 2)) * db
                    found.append((self.device(a, b, self.c, self.core), a + 4 * lax.rem(b, 2), self.kind_of(a, b)))
        return found

    def across(self):
        return self.device(self.a, 3 - self.b, self.c, self.core)

    def along(self, step):
        return self.device(self.a, self.b, lax.rem(self.c + step, 4), self.core)

    def twin(self):
        return self.device(self.a, self.b, self.c, 1 - self.core)


def columns(head):
    return pl.ds(pl.multiple_of(head * HD, HD), HD)


def rows(start, size):
    return pl.ds(pl.multiple_of(start, 16), size)


def send(src, dst, send_sem, recv_sem, device):
    pltpu.make_async_remote_copy(
        src_ref=src, dst_ref=dst, send_sem=send_sem, recv_sem=recv_sem, device_id=device, device_id_type=MESH
    ).start()


def wait_bytes(ref, sem):
    pltpu.make_async_copy(ref, ref, sem).wait()


def kernel(
    q_ref, k_ref, v_ref, dq_ref, dk_ref, dv_ref, out_ref,
    q_own, k_own, q_all, k_all, o_all,
    stage_sem, q_send, q_recv, k1_send, k1_recv, k2_send, across_recv, along_recv, twin_recv, o_send, o_recv,
):
    ctx, uly = lax.axis_index("ctx"), lax.axis_index("uly")
    core = lax.rem(ctx, 2)
    xyz = (lax.rem(uly, 4), lax.div(uly, 4) * 2 + lax.rem(lax.div(ctx, 2), 2), lax.div(ctx, 4))
    places = [Place(slot, xyz, core) for slot in range(SLOTS)]

    staged = [
        pltpu.make_async_copy(ref, k_own.at[at], stage_sem.at[at]) for at, ref in enumerate((k_ref, dk_ref, v_ref, dv_ref))
    ] + [pltpu.make_async_copy(ref, q_own.at[at], stage_sem.at[4 + at]) for at, ref in enumerate((q_ref, dq_ref))]
    for copy in staged:
        copy.start()

    barrier = pltpu.get_barrier_semaphore()
    partners = [places[0].twin()]
    for slot, place in enumerate(places):
        if LAYOUT[slot] not in LAYOUT[:slot]:
            partners += [device for device, _, _ in place.peers()]
            partners += [place.across()] + [place.along(step) for step in (1, 2, 3)]
    for device in partners:
        pl.semaphore_signal(barrier, inc=1, device_id=device, device_id_type=MESH)
    pl.semaphore_wait(barrier, len(partners))
    for copy in staged:
        copy.wait()

    def send_keys(slot):
        place = places[slot]
        there = k_all.at[slot, :, rows(place.block * BLOCK + place.member * KROWS, KROWS), :]
        for device, _, kind in place.peers():
            send(k_own.at[:, :, columns(slot * GROUP + kind)], there, k1_send.at[slot], k1_recv.at[slot], device)
        pltpu.make_async_copy(k_own.at[:, :, columns(slot * GROUP + place.kind)], there, k1_recv.at[slot]).start()

    def send_queries(slot):
        place = places[slot]
        there = q_all.at[slot, :, rows(place.member * QROWS, QROWS), :]
        for device, _, kind in place.peers():
            send(q_own.at[:, :, columns(slot * GROUP + kind)], there, q_send.at[slot], q_recv.at[slot], device)
        pltpu.make_async_copy(q_own.at[:, :, columns(slot * GROUP + place.kind)], there, q_recv.at[slot]).start()

    def block_ref(slot, block):
        return k_all.at[slot, :, rows(block * BLOCK, BLOCK), :]

    def to_twin(slot, block):
        ref = block_ref(slot, block)
        send(ref, ref, k2_send.at[slot], twin_recv.at[slot], places[slot].twin())

    def along(slot, block, which, step):
        ref = block_ref(slot, block)
        hop = (1, 3)[which] if step == 2 else step
        send(ref, ref, k2_send.at[slot], along_recv.at[slot, which, step - 1], places[slot].along(hop))

    def own(slot):
        place = places[slot]
        ref = block_ref(slot, place.block)
        wait_bytes(ref, k1_recv.at[slot])
        send(ref, ref, k2_send.at[slot], across_recv.at[slot], place.across())
        along(slot, place.block, 0, 1)
        along(slot, place.block, 0, 3)
        to_twin(slot, place.block)

    def cross(slot):
        place = places[slot]
        block = place.block_of(3 - place.b, place.c, core)
        wait_bytes(block_ref(slot, block), across_recv.at[slot])
        along(slot, block, 1, 3)
        along(slot, block, 1, 1)
        to_twin(slot, block)

    def arrived(slot, which, step):
        place = places[slot]
        b = 3 - place.b if which else place.b
        block = place.block_of(b, lax.rem(place.c + 4 - step, 4), core)
        wait_bytes(block_ref(slot, block), along_recv.at[slot, which, step - 1])
        if step == (1, 3)[which]:
            along(slot, block, which, 2)
        to_twin(slot, block)

    def near(slot):
        arrived(slot, 0, 1)
        arrived(slot, 0, 3)
        arrived(slot, 1, 3)
        arrived(slot, 1, 1)

    def far(slot):
        arrived(slot, 0, 2)
        arrived(slot, 1, 2)

    def ready(slot):
        wait_bytes(k_all.at[slot, :, : KEYS // 2, :], twin_recv.at[slot])
        wait_bytes(q_all.at[slot], q_recv.at[slot])

    steps = {"keys": send_keys, "queries": send_queries, "own": own, "cross": cross, "near": near, "far": far, "ready": ready}

    def follow(plan):
        for step in plan.split():
            steps[step[:-1]](int(step[-1]))

    def attend(slot):
        def tile(at, _):
            for point in range(1, QUERIES // TILE):
                if PLAN[slot + 1][point]:
                    pl.when(at == point)(functools.partial(follow, PLAN[slot + 1][point]))
            here = rows(at * TILE, TILE)
            query, dquery = q_all[slot, 0, here, :], q_all[slot, 1, here, :]
            key, dkey = k_all[slot, 0], k_all[slot, 1]
            value, dvalue = k_all[slot, 2], k_all[slot, 3]
            scores = scores_of(query, key) * SCALE_LOG2
            tangents = scores_of(jnp.concatenate([dquery, query], 1), jnp.concatenate([key, dkey], 1))
            highest = jnp.max(scores, axis=1, keepdims=True)
            weights = jnp.exp2(scores - highest)
            total = jnp.sum(weights, axis=1, keepdims=True)
            weights_rounded = weights.astype(jnp.bfloat16)
            product = weights * (tangents * SCALE)
            both = mix(weights_rounded, jnp.concatenate([value, dvalue], 1))
            mixed = both[:, :HD] / total
            summed = mix(product.astype(jnp.bfloat16), jnp.concatenate([value, jnp.ones_like(value)], 1))
            tangent = (summed[:, :HD] + both[:, HD:] - mixed * summed[:, HD:]) / total
            o_all[slot, 0, here, :] = mixed.astype(jnp.bfloat16)
            o_all[slot, 1, here, :] = tangent.astype(jnp.bfloat16)
            send_outputs(slot, at)
            return 0

        lax.fori_loop(0, QUERIES // TILE, tile, 0)

    def send_outputs(slot, at):
        place = places[slot]
        there = out_ref.at[:, :, columns(slot * GROUP + place.kind)]
        for member in [at * (TILE // QROWS) + part for part in range(TILE // QROWS)]:
            here = o_all.at[slot, :, rows(member * QROWS, QROWS), :]
            device = place.device(lax.rem(member, 4), lax.div(place.b, 2) * 2 + lax.div(member, 4), place.c, core)

            @pl.when(member != place.member)
            def _():
                send(here, there, o_send.at[slot], o_recv, device)

            @pl.when(member == place.member)
            def _():
                pltpu.make_async_copy(here, there, o_recv).start()

    follow(PLAN[0][0])
    for slot in range(SLOTS):
        follow(PLAN[slot + 1][0])
        attend(slot)

    for slot in range(SLOTS):
        wait_bytes(k_all.at[slot, :, : 7 * KROWS, :], k1_send.at[slot])
        wait_bytes(q_all.at[slot, :, : 7 * QROWS, :], q_send.at[slot])
        wait_bytes(k_all.at[slot, :, : 15 * BLOCK, :], k2_send.at[slot])
        wait_bytes(o_all.at[slot, :, : 7 * QROWS, :], o_send.at[slot])
    wait_bytes(out_ref, o_recv)


def on_device(query_rows, key_rows, value_rows, query_tangent, key_tangent, value_tangent):
    dma = pltpu.SemaphoreType.DMA
    out = pl.pallas_call(
        kernel,
        out_shape=jax.ShapeDtypeStruct((2, QROWS, COLS), jnp.bfloat16),
        in_specs=[pl.BlockSpec(memory_space=pl.ANY)] * 6,
        out_specs=pl.BlockSpec(memory_space=pl.ANY),
        scratch_shapes=[
            pltpu.VMEM((2, QROWS, COLS), jnp.bfloat16),
            pltpu.VMEM((4, KROWS, COLS), jnp.bfloat16),
            pltpu.VMEM((SLOTS, 2, QUERIES, HD), jnp.bfloat16),
            pltpu.VMEM((SLOTS, 4, KEYS, HD), jnp.bfloat16),
            pltpu.VMEM((SLOTS, 2, QUERIES, HD), jnp.bfloat16),
            dma((6,)),
            dma((SLOTS,)),
            dma((SLOTS,)),
            dma((SLOTS,)),
            dma((SLOTS,)),
            dma((SLOTS,)),
            dma((SLOTS,)),
            dma((SLOTS, 2, 3)),
            dma((SLOTS,)),
            dma((SLOTS,)),
            dma(()),
        ],
        compiler_params=pltpu.CompilerParams(collective_id=0, has_side_effects=True, vmem_limit_bytes=56 * 2**20),
        cost_estimate=pl.CostEstimate(flops=16_000_000_000, bytes_accessed=6_000_000, transcendentals=10_500_000),
        name="tangent_attention",
    )(query_rows, key_rows, value_rows, query_tangent, key_tangent, value_tangent)
    return out[0], out[1]


def solution(mesh):
    whole = P(("ctx", "uly"), None)
    return jax.shard_map(on_device, mesh=mesh, in_specs=(whole,) * 6, out_specs=(whole, whole), check_vma=False)
```

```python
import functools
import math

import jax
import jax.numpy as jnp
from jax import lax
from jax.experimental import pallas as pl
from jax.experimental.pallas import tpu as pltpu
from jax.sharding import PartitionSpec as P

HD = 128
SLOTS = 5
GROUP = 8
QROWS = 128
KROWS = 16
BLOCK = GROUP * KROWS
QUERIES = GROUP * QROWS
KEYS = 2048
COLS = 5120
TILE = 256
SCALE = 1.0 / math.sqrt(HD)
SCALE_LOG2 = SCALE * math.log2(math.e)
MESH = pl.DeviceIdType.MESH

LAYOUT = (
    (2, 0, 1, 0),
    (1, 2, 0, 0),
    (0, 1, 2, 0),
    (1, 2, 0, 1),
    (0, 1, 2, 1),
)

PLAN = (
    (
        " ".join(("keys0 keys1 keys2", "keys3 keys4")),
        " ".join(("queries0 own0 own1 own2", "own3 own4 cross0 cross1", "near0 cross2 cross3 near1", "cross4 far0 near2 near3", "far1")),
    ),
    ("queries1 ready0", "near4", "queries2 far2", "far3",),
    ("queries3 ready1", "far4", "queries4", "",),
    ("ready2", "", "", "",),
    ("ready3", "", "", "",),
    ("ready4", "", "", "",),
)


def scores_of(left, right):
    return lax.dot_general(left, right, (((1,), (1,)), ((), ())), preferred_element_type=jnp.float32)


def mix(left, right):
    return jnp.dot(left, right, preferred_element_type=jnp.float32)


class Place:
    def __init__(self, slot, xyz, core):
        ring, pair, keys, shift = LAYOUT[slot]
        self.order, self.shift, self.core, self.slot = (ring, pair, keys), shift, core, slot
        self.a = xyz[ring]
        self.b = lax.rem(xyz[pair] + shift, 4)
        self.c = xyz[keys]
        self.member = self.a + 4 * lax.rem(self.b, 2)
        self.kind = self.kind_of(self.a, self.b)
        self.block = self.block_of(self.b, self.c, core)

    def kind_of(self, a, b):
        return a + 4 * lax.rem(lax.rem(b, 2) + lax.div(b, 2), 2)

    def block_of(self, b, c, core):
        return (c * 2 + lax.div(b, 2)) * 2 + core

    def device(self, a, b, c, core):
        xyz = [None] * 3
        for axis, at in zip(self.order, (a, lax.rem(b + 4 - self.shift, 4), c)):
            xyz[axis] = at
        x, y, z = xyz
        return (z * 4 + lax.rem(y, 2) * 2 + core, lax.div(y, 2) * 4 + x)

    def peers(self):
        found = []
        for da in range(4):
            for db in range(2):
                if da or db:
                    a = lax.rem(self.a + da, 4)
                    b = self.b + (1 - 2 * lax.rem(self.b, 2)) * db
                    found.append((self.device(a, b, self.c, self.core), a + 4 * lax.rem(b, 2), self.kind_of(a, b)))
        return found

    def across(self):
        return self.device(self.a, 3 - self.b, self.c, self.core)

    def along(self, step):
        return self.device(self.a, self.b, lax.rem(self.c + step, 4), self.core)

    def twin(self):
        return self.device(self.a, self.b, self.c, 1 - self.core)


def columns(head):
    return pl.ds(pl.multiple_of(head * HD, HD), HD)


def rows(start, size):
    return pl.ds(pl.multiple_of(start, 16), size)


def send(src, dst, send_sem, recv_sem, device):
    pltpu.make_async_remote_copy(
        src_ref=src, dst_ref=dst, send_sem=send_sem, recv_sem=recv_sem, device_id=device, device_id_type=MESH
    ).start()


def wait_bytes(ref, sem):
    pltpu.make_async_copy(ref, ref, sem).wait()


def kernel(
    q_ref, k_ref, v_ref, dq_ref, dk_ref, dv_ref, out_ref,
    q_own, k_own, q_all, k_all, o_all,
    stage_sem, q_send, q_recv, k1_send, k1_recv, k2_send, across_recv, along_recv, twin_recv, o_send, o_recv,
):
    ctx, uly = lax.axis_index("ctx"), lax.axis_index("uly")
    core = lax.rem(ctx, 2)
    xyz = (lax.rem(uly, 4), lax.div(uly, 4) * 2 + lax.rem(lax.div(ctx, 2), 2), lax.div(ctx, 4))
    places = [Place(slot, xyz, core) for slot in range(SLOTS)]

    staged = [
        pltpu.make_async_copy(ref, k_own.at[at], stage_sem.at[at]) for at, ref in enumerate((k_ref, dk_ref, v_ref, dv_ref))
    ] + [pltpu.make_async_copy(ref, q_own.at[at], stage_sem.at[4 + at]) for at, ref in enumerate((q_ref, dq_ref))]
    for copy in staged:
        copy.start()

    barrier = pltpu.get_barrier_semaphore()
    partners = [places[0].twin()]
    for slot, place in enumerate(places):
        if LAYOUT[slot] not in LAYOUT[:slot]:
            partners += [device for device, _, _ in place.peers()]
            partners += [place.across()] + [place.along(step) for step in (1, 2, 3)]
    for device in partners:
        pl.semaphore_signal(barrier, inc=1, device_id=device, device_id_type=MESH)
    pl.semaphore_wait(barrier, len(partners))
    for copy in staged[:4]:
        copy.wait()

    def send_keys(slot):
        place = places[slot]
        there = k_all.at[slot, :, rows(place.block * BLOCK + place.member * KROWS, KROWS), :]
        for device, _, kind in place.peers():
            send(k_own.at[:, :, columns(slot * GROUP + kind)], there, k1_send.at[slot], k1_recv.at[slot], device)
        pltpu.make_async_copy(k_own.at[:, :, columns(slot * GROUP + place.kind)], there, k1_recv.at[slot]).start()

    def send_queries(slot):
        place = places[slot]
        there = q_all.at[slot, :, rows(place.member * QROWS, QROWS), :]
        for device, _, kind in place.peers():
            send(q_own.at[:, :, columns(slot * GROUP + kind)], there, q_send.at[slot], q_recv.at[slot], device)
        pltpu.make_async_copy(q_own.at[:, :, columns(slot * GROUP + place.kind)], there, q_recv.at[slot]).start()

    def block_ref(slot, block):
        return k_all.at[slot, :, rows(block * BLOCK, BLOCK), :]

    def to_twin(slot, block):
        ref = block_ref(slot, block)
        send(ref, ref, k2_send.at[slot], twin_recv.at[slot], places[slot].twin())

    def along(slot, block, which, step):
        ref = block_ref(slot, block)
        hop = (1, 3)[which] if step == 2 else step
        send(ref, ref, k2_send.at[slot], along_recv.at[slot, which, step - 1], places[slot].along(hop))

    def own(slot):
        place = places[slot]
        ref = block_ref(slot, place.block)
        wait_bytes(ref, k1_recv.at[slot])
        send(ref, ref, k2_send.at[slot], across_recv.at[slot], place.across())
        along(slot, place.block, 0, 1)
        along(slot, place.block, 0, 3)
        to_twin(slot, place.block)

    def cross(slot):
        place = places[slot]
        block = place.block_of(3 - place.b, place.c, core)
        wait_bytes(block_ref(slot, block), across_recv.at[slot])
        along(slot, block, 1, 3)
        along(slot, block, 1, 1)
        to_twin(slot, block)

    def arrived(slot, which, step):
        place = places[slot]
        b = 3 - place.b if which else place.b
        block = place.block_of(b, lax.rem(place.c + 4 - step, 4), core)
        wait_bytes(block_ref(slot, block), along_recv.at[slot, which, step - 1])
        if step == (1, 3)[which]:
            along(slot, block, which, 2)
        to_twin(slot, block)

    def near(slot):
        arrived(slot, 0, 1)
        arrived(slot, 0, 3)
        arrived(slot, 1, 3)
        arrived(slot, 1, 1)

    def far(slot):
        arrived(slot, 0, 2)
        arrived(slot, 1, 2)

    def ready(slot):
        wait_bytes(k_all.at[slot, :, : KEYS // 2, :], twin_recv.at[slot])
        wait_bytes(q_all.at[slot], q_recv.at[slot])

    steps = {"keys": send_keys, "queries": send_queries, "own": own, "cross": cross, "near": near, "far": far, "ready": ready}

    def follow(plan):
        for step in plan.split():
            steps[step[:-1]](int(step[-1]))

    def attend(slot):
        def tile(at, _):
            for point in range(1, QUERIES // TILE):
                if PLAN[slot + 1][point]:
                    pl.when(at == point)(functools.partial(follow, PLAN[slot + 1][point]))
            here = rows(at * TILE, TILE)
            query, dquery = q_all[slot, 0, here, :], q_all[slot, 1, here, :]
            key, dkey = k_all[slot, 0], k_all[slot, 1]
            value, dvalue = k_all[slot, 2], k_all[slot, 3]
            scores = scores_of(query, key) * SCALE_LOG2
            tangents = scores_of(jnp.concatenate([dquery, query], 1), jnp.concatenate([key, dkey], 1))
            highest = jnp.max(scores, axis=1, keepdims=True)
            weights = jnp.exp2(scores - highest)
            total = jnp.sum(weights, axis=1, keepdims=True)
            weights_rounded = weights.astype(jnp.bfloat16)
            product = weights * (tangents * SCALE)
            both = mix(weights_rounded, jnp.concatenate([value, dvalue], 1))
            mixed = both[:, :HD] / total
            summed = mix(product.astype(jnp.bfloat16), jnp.concatenate([value, jnp.ones_like(value)], 1))
            tangent = (summed[:, :HD] + both[:, HD:] - mixed * summed[:, HD:]) / total
            o_all[slot, 0, here, :] = mixed.astype(jnp.bfloat16)
            o_all[slot, 1, here, :] = tangent.astype(jnp.bfloat16)
            send_outputs(slot, at)
            return 0

        lax.fori_loop(0, QUERIES // TILE, tile, 0)

    def send_outputs(slot, at):
        place = places[slot]
        there = out_ref.at[:, :, columns(slot * GROUP + place.kind)]
        for member in [at * (TILE // QROWS) + part for part in range(TILE // QROWS)]:
            here = o_all.at[slot, :, rows(member * QROWS, QROWS), :]
            device = place.device(lax.rem(member, 4), lax.div(place.b, 2) * 2 + lax.div(member, 4), place.c, core)

            @pl.when(member != place.member)
            def _():
                send(here, there, o_send.at[slot], o_recv, device)

            @pl.when(member == place.member)
            def _():
                pltpu.make_async_copy(here, there, o_recv).start()

    follow(PLAN[0][0])
    for copy in staged[4:]:
        copy.wait()
    follow(PLAN[0][1])
    for slot in range(SLOTS):
        follow(PLAN[slot + 1][0])
        attend(slot)

    for slot in range(SLOTS):
        wait_bytes(k_all.at[slot, :, : 7 * KROWS, :], k1_send.at[slot])
        wait_bytes(q_all.at[slot, :, : 7 * QROWS, :], q_send.at[slot])
        wait_bytes(k_all.at[slot, :, : 15 * BLOCK, :], k2_send.at[slot])
        wait_bytes(o_all.at[slot, :, : 7 * QROWS, :], o_send.at[slot])
    wait_bytes(out_ref, o_recv)


def on_device(query_rows, key_rows, value_rows, query_tangent, key_tangent, value_tangent):
    dma = pltpu.SemaphoreType.DMA
    out = pl.pallas_call(
        kernel,
        out_shape=jax.ShapeDtypeStruct((2, QROWS, COLS), jnp.bfloat16),
        in_specs=[pl.BlockSpec(memory_space=pl.ANY)] * 6,
        out_specs=pl.BlockSpec(memory_space=pl.ANY),
        scratch_shapes=[
            pltpu.VMEM((2, QROWS, COLS), jnp.bfloat16),
            pltpu.VMEM((4, KROWS, COLS), jnp.bfloat16),
            pltpu.VMEM((SLOTS, 2, QUERIES, HD), jnp.bfloat16),
            pltpu.VMEM((SLOTS, 4, KEYS, HD), jnp.bfloat16),
            pltpu.VMEM((SLOTS, 2, QUERIES, HD), jnp.bfloat16),
            dma((6,)),
            dma((SLOTS,)),
            dma((SLOTS,)),
            dma((SLOTS,)),
            dma((SLOTS,)),
            dma((SLOTS,)),
            dma((SLOTS,)),
            dma((SLOTS, 2, 3)),
            dma((SLOTS,)),
            dma((SLOTS,)),
            dma(()),
        ],
        compiler_params=pltpu.CompilerParams(collective_id=0, has_side_effects=True, vmem_limit_bytes=56 * 2**20),
        cost_estimate=pl.CostEstimate(flops=16_000_000_000, bytes_accessed=6_000_000, transcendentals=10_500_000),
        name="tangent_attention",
    )(query_rows, key_rows, value_rows, query_tangent, key_tangent, value_tangent)
    return out[0], out[1]


def solution(mesh):
    whole = P(("ctx", "uly"), None)
    return jax.shard_map(on_device, mesh=mesh, in_specs=(whole,) * 6, out_specs=(whole, whole), check_vma=False)
```
